128 devices in a mesh: dap: 32 (over z, x_lo, y), rep: 4 (over x_hi, core).
Axes of the slice: x: 4 (x_hi: 2, x_lo: 2; x = x_hi * 2 + x_lo), y: 4, z: 4, core: 2. Of those that a mesh axis runs over, the one named last changes fastest.
Arguments:
- pair_rep: bfloat16 [1024, 1024, 128], P('dap'), may hold values from -6 to 6
- residue_mask: int32 [1024], replicated, may hold values 0 or 1
- pair_mask: int32 [1024, 1024], P('dap'), may hold values 0 or 1
- input_gain: float32 [128], replicated, may hold values from 0.25 to 1.75
- input_bias: float32 [128], replicated, may hold values from -3 to 3
- left_proj: bfloat16 [128, 128], P(None, 'rep'), may hold values from -0.5 to 0.5
- left_gate: bfloat16 [128, 128], P(None, 'rep'), may hold values from -0.5 to 0.5
- right_proj: bfloat16 [128, 128], P(None, 'rep'), may hold values from -0.5 to 0.5
- right_gate: bfloat16 [128, 128], P(None, 'rep'), may hold values from -0.5 to 0.5
- gate_weight: bfloat16 [128, 128], P(None, 'rep'), may hold values from -0.5 to 0.5
- output_gain: float32 [128], replicated, may hold values from 0.25 to 1.75
- output_bias: float32 [128], replicated, may hold values from -3 to 3
- out_weight: bfloat16 [128, 128], replicated, may hold values from -0.5 to 0.5
Outputs:
- update: bfloat16 [128, 1024, 1024], P('rep', None, 'dap')
The draws below stay inside these ranges and needn't reach their ends.
All inputs are finite; a program needn't handle non-finite values. No bound on the sum of `pair_mask` on one device may be relied on, other than what follows from the above.
Results may differ from the reference program's by a relative error of at most 0.0066.
Values may be sent and summed in bfloat16 or wider, within the bound.
No kernel may reach another device: no remote copies, remote signals or barrier semaphores. Data moves between devices by JAX's collectives and lax.ppermute only.
A program may use at most 192 MiB of HBM per device.

```python
import jax
import jax.numpy as jnp
from jax import lax

C = 128
H = 128
N = 1024


def place_ends(array, stream_key, smallest, high):
    extent = array.shape
    place = [jax.random.randint(jax.random.fold_in(stream_key, axis), (), 0, extent[axis]) for axis in range(len(extent))]
    array = array.at[tuple(place)].set(smallest)
    longest = extent.index(max(extent))
    place[longest] = (place[longest] + 1) % extent[longest]
    return array.at[tuple(place)].set(high)


def level_of(own_key, extent, pieces, smallest, high):
    level, own = 1.0, jax.random.fold_in(own_key, 6)
    for axis_at, blocks in pieces:
        steps = jnp.exp(jax.random.uniform(jax.random.fold_in(own, axis_at), (blocks,), jnp.float32, smallest / len(pieces), high / len(pieces)))
        level = level * jnp.repeat(steps, extent[axis_at] // blocks).reshape([-1 if axis == axis_at else 1 for axis in range(len(extent))])
    return level


def gaussian(stream_key, shape, spread, bound, pieces=(), held_as=jnp.bfloat16):
    factor_of = level_of(stream_key, shape, pieces, -0.22, 0.18) if pieces else 1.0
    values = jax.random.normal(stream_key, shape, jnp.float32) * spread * factor_of
    return jnp.minimum(jnp.maximum(values, -bound), bound).astype(held_as)


def setup_inputs(seed: int = 0) -> dict:
    arg_keys = jax.random.split(jax.random.key(seed), 14)
    return {
        "pair_rep": gaussian(arg_keys[0], (N, N, C), 1.0, 6.0, ((0, 32),)),
        "residue_mask": place_ends((jax.random.randint(arg_keys[1], (N,), 0, 16) < 15).astype(jnp.int32), jax.random.fold_in(arg_keys[1], 1), 0, 1),
        "pair_mask": place_ends((jax.random.randint(arg_keys[2], (N, N), 0, 8) < 7).astype(jnp.int32), jax.random.fold_in(arg_keys[2], 1), 0, 1),
        "input_gain": jnp.clip(1.0 + 0.15 * jax.random.normal(arg_keys[3], (C,), jnp.float32), 0.25, 1.75),
        "input_bias": gaussian(arg_keys[4], (C,), 0.5, 3.0, (), jnp.float32),
        "left_proj": gaussian(arg_keys[5], (C, H), C ** -0.5, 0.5, ((1, 4),)),
        "left_gate": gaussian(arg_keys[6], (C, H), C ** -0.5, 0.5, ((1, 4),)),
        "right_proj": gaussian(arg_keys[7], (C, H), C ** -0.5, 0.5, ((1, 4),)),
        "right_gate": gaussian(arg_keys[8], (C, H), C ** -0.5, 0.5, ((1, 4),)),
        "gate_weight": gaussian(arg_keys[9], (C, C), C ** -0.5, 0.5, ((1, 4),)),
        "output_gain": jnp.clip(1.0 + 0.15 * jax.random.normal(arg_keys[10], (H,), jnp.float32), 0.25, 1.75),
        "output_bias": gaussian(arg_keys[11], (H,), 0.5, 3.0, (), jnp.float32),
        "out_weight": gaussian(arg_keys[12], (H, C), H ** -0.5, 0.5),
    }


eps = 1e-05

def channel_norm(values, gain, bias, axis):
    mean = lax.optimization_barrier(jnp.mean(values, axis=axis, keepdims=True))
    centred = values - mean
    var = lax.optimization_barrier(jnp.mean(centred * centred, axis=axis, keepdims=True))
    return centred * jax.lax.rsqrt(var + eps) * gain + bias

def reference(pair_rep, residue_mask, pair_mask, input_gain, input_bias, left_proj, left_gate, right_proj, right_gate, gate_weight, output_gain, output_bias, out_weight):
    normed_in = channel_norm(pair_rep.astype(jnp.float32), input_gain, input_bias, -1).astype(jnp.bfloat16)
    flat = normed_in.reshape(N * N, C)
    weights = (residue_mask[:, None] * residue_mask[None, :] * pair_mask).astype(jnp.float32)

    def project(proj_weight, gate_proj):
        linear = jnp.dot(flat, proj_weight, preferred_element_type=jnp.float32)
        gated = jax.nn.sigmoid(jnp.dot(flat, gate_proj, preferred_element_type=jnp.float32))
        result = (gated * linear).reshape(N, N, H) * weights[:, :, None]
        return jnp.transpose(result.astype(jnp.bfloat16), (2, 0, 1))
    left = project(left_proj, left_gate)
    right = project(right_proj, right_gate)
    gating = jax.nn.sigmoid(jnp.dot(flat, gate_weight, preferred_element_type=jnp.float32))
    gating = jnp.transpose(gating.reshape(N, N, C), (2, 0, 1)).astype(jnp.bfloat16)
    product = jnp.einsum('cik,cjk->cij', left.astype(jnp.float32), right.astype(jnp.float32)).astype(jnp.bfloat16)
    normed_out = channel_norm(product.astype(jnp.float32), output_gain[:, None, None], output_bias[:, None, None], 0).astype(jnp.bfloat16)
    projected = jnp.einsum('hij,hc->cij', normed_out.astype(jnp.float32), out_weight.astype(jnp.float32))
    return (gating.astype(jnp.float32) * projected).astype(jnp.bfloat16)
```

```python
import jax
import jax.numpy as jnp
from jax import lax
from jax.experimental import pallas as pl
from jax.experimental.pallas import tpu as pltpu
from jax.sharding import PartitionSpec as P

eps = 1e-05
bf16 = jnp.bfloat16
f32 = jnp.float32
everyone = ("dap", "rep")
lane = 128


def params(mib=48):
    return pltpu.CompilerParams(vmem_limit_bytes=mib * 2**20)


def sigmoid(x):
    return 0.5 * jnp.tanh(0.5 * x) + 0.5


def rows_by_rows(a, b):
    return lax.dot_general(a, b, (((1,), (1,)), ((), ())), preferred_element_type=f32)


def norm_kernel(where, x_ref, gain_ref, bias_ref, out_ref):
    x = x_ref[...].astype(f32)
    width = x.shape[-1]
    mean = jnp.sum(x, axis=-1, keepdims=True) * (1.0 / width)
    centred = x - mean
    var = jnp.sum(centred * centred, axis=-1, keepdims=True) * (1.0 / width)
    out_ref[...] = (centred * lax.rsqrt(var + eps) * gain_ref[...] + bias_ref[...]).astype(bf16)


def norm_in(where, pair_rep, gain, bias, share, tile):
    rows, total, width = pair_rep.shape
    return pl.pallas_call(
        norm_kernel,
        grid_spec=pltpu.PrefetchScalarGridSpec(
            num_scalar_prefetch=1,
            grid=(total // tile,),
            in_specs=[
                pl.BlockSpec((share, tile, width), lambda t, where: (where[1], t, 0)),
                pl.BlockSpec((1, 1, width), lambda t, where: (0, 0, 0)),
                pl.BlockSpec((1, 1, width), lambda t, where: (0, 0, 0)),
            ],
            out_specs=pl.BlockSpec((share, tile, width), lambda t, where: (0, t, 0)),
        ),
        out_shape=jax.ShapeDtypeStruct((share, total, width), bf16),
        compiler_params=params(),
        name="norm_in",
    )(where, pair_rep, gain.reshape(1, 1, width), bias.reshape(1, 1, width))


def project_kernel(where, residues, x_ref, w_ref, keep_ref, mask_ref, out_ref, held):
    share, tile, width = x_ref.shape
    hidden = out_ref.shape[0]
    lanes = mask_ref[...].astype(f32)
    keep = keep_ref[...].astype(f32) * lanes
    first = where[0] * share
    for i in range(share):
        x = x_ref[i]
        weight = keep[i : i + 1, :] * residues[first + i].astype(f32)
        for side in range(2):
            linear = rows_by_rows(w_ref[:, 2 * side].reshape(hidden, width), x)
            gate = rows_by_rows(w_ref[:, 2 * side + 1].reshape(hidden, width), x)
            result = sigmoid(gate) * linear * weight
            for part in range(tile // lane):
                held[side, part, pl.ds(i, hidden, stride=share), :] = result[
                    :, part * lane : (part + 1) * lane
                ]
    for side in range(2):
        for part in range(tile // lane):
            out_ref[
                :, side * share : (side + 1) * share, part * lane : (part + 1) * lane
            ] = held[side, part].reshape(hidden, share, lane).astype(bf16)


def project(where, residue_mask, normed, weights, pair_mask, tile):
    share, total, width = normed.shape
    hidden = weights.shape[0] * weights.shape[2]
    return pl.pallas_call(
        project_kernel,
        grid_spec=pltpu.PrefetchScalarGridSpec(
            num_scalar_prefetch=2,
            grid=(total // tile,),
            in_specs=[
                pl.BlockSpec((share, tile, width), lambda t, *_: (0, t, 0)),
                pl.BlockSpec(weights.shape, lambda t, *_: (0, 0, 0, 0)),
                pl.BlockSpec((share, tile), lambda t, where, _: (where[1], t)),
                pl.BlockSpec((1, tile), lambda t, *_: (0, t)),
            ],
            out_specs=pl.BlockSpec((hidden, 2 * share, tile), lambda t, *_: (0, 0, t)),
            scratch_shapes=[pltpu.VMEM((2, tile // lane, hidden * share, lane), f32)],
        ),
        out_shape=jax.ShapeDtypeStruct((hidden, 2 * share, total), bf16),
        compiler_params=params(),
        name="project",
    )(where, residue_mask, normed, weights, pair_mask, residue_mask.reshape(1, total))


def gate_kernel(x_ref, w_ref, out_ref):
    width = x_ref.shape[-1]
    w = w_ref[:, 4].reshape(-1, width)
    for i in range(x_ref.shape[0]):
        out_ref[i] = sigmoid(rows_by_rows(w, x_ref[i])).astype(bf16)


def gates(normed, weights, tile):
    share, total, width = normed.shape
    channels = weights.shape[0] * weights.shape[2]
    return pl.pallas_call(
        gate_kernel,
        grid=(total // tile,),
        in_specs=[
            pl.BlockSpec((share, tile, width), lambda t: (0, t, 0)),
            pl.BlockSpec(weights.shape, lambda t: (0, 0, 0, 0)),
        ],
        out_specs=pl.BlockSpec((share, channels, tile), lambda t: (0, 0, t)),
        out_shape=jax.ShapeDtypeStruct((share, channels, total), bf16),
        compiler_params=params(),
        cost_estimate=pl.CostEstimate(
            flops=2 * share * total * width * channels,
            bytes_accessed=4 * share * total * width,
            transcendentals=share * total * channels,
        ),
        name="gates",
    )(normed, weights)


def product_kernel(left_ref, right_ref, out_ref):
    blocks, two, total = left_ref.shape
    share = two // 2
    left = left_ref[:, :share, :].reshape(blocks * share, total)
    right = right_ref[:, share:, :].reshape(-1, total)
    out_ref[...] = rows_by_rows(left, right).astype(bf16).reshape(out_ref.shape)


def products(both, tile):
    blocks, two, total = both.shape
    return pl.pallas_call(
        product_kernel,
        grid=(blocks // tile,),
        in_specs=[
            pl.BlockSpec((tile, two, total), lambda t: (t, 0, 0)),
            pl.BlockSpec(both.shape, lambda t: (0, 0, 0)),
        ],
        out_specs=pl.BlockSpec((tile, two // 2, total), lambda t: (t, 0, 0)),
        out_shape=jax.ShapeDtypeStruct((blocks, two // 2, total), bf16),
        compiler_params=params(),
        name="products",
    )(both, both)


def update_kernel(p_ref, gate_ref, gain_ref, bias_ref, w_ref, out_ref, held, placed):
    hidden, share, tile = p_ref.shape
    channels = w_ref.shape[0]
    pack, span = 4, tile // 4
    values = p_ref[...].astype(f32)
    mean = jnp.sum(values, axis=0, keepdims=True) * (1.0 / hidden)
    centred = values - mean
    var = jnp.sum(centred * centred, axis=0, keepdims=True) * (1.0 / hidden)
    normed = centred * lax.rsqrt(var + eps) * gain_ref[...] + bias_ref[...]
    held[...] = normed.reshape(hidden * share, tile)
    for i in range(share):
        row = held[pl.ds(i, hidden, stride=share), :].astype(bf16)
        projected = jnp.dot(w_ref[...], row, preferred_element_type=f32)
        placed[pl.ds(i, channels, stride=share), :] = gate_ref[i].astype(f32) * projected
    result = placed[...].reshape(channels // pack, pack, share, tile)
    for block in range(pack):
        piece = jnp.concatenate(
            [result[:, c, :, block * span : (block + 1) * span] for c in range(pack)], axis=-1
        )
        out_ref[block] = piece.astype(bf16).reshape(out_ref.shape[1:])


def updates(product, gating, gain, bias, out_weight_t):
    hidden, share, total = product.shape
    channels = out_weight_t.shape[0]
    tile = 128
    rows = channels * share // 4
    return pl.pallas_call(
        update_kernel,
        grid=(total // tile,),
        in_specs=[
            pl.BlockSpec((hidden, share, tile), lambda t: (0, 0, t)),
            pl.BlockSpec((share, channels, tile), lambda t: (0, 0, t)),
            pl.BlockSpec((hidden, 1, 1), lambda t: (0, 0, 0)),
            pl.BlockSpec((hidden, 1, 1), lambda t: (0, 0, 0)),
            pl.BlockSpec((channels, hidden), lambda t: (0, 0)),
        ],
        out_specs=pl.BlockSpec((4, rows, tile), lambda t: (t, 0, 0)),
        out_shape=jax.ShapeDtypeStruct((total // 32, rows, tile), bf16),
        scratch_shapes=[
            pltpu.VMEM((hidden * share, tile), f32),
            pltpu.VMEM((channels * share, tile), f32),
        ],
        compiler_params=params(),
        name="updates",
    )(product, gating, gain.reshape(hidden, 1, 1), bias.reshape(hidden, 1, 1), out_weight_t)


def place_kernel(u_ref, out_ref):
    blocks, share, lanes = u_ref.shape
    flat = u_ref[...].astype(f32).reshape(blocks * share, lanes)
    out_ref[...] = flat.T.astype(bf16).reshape(out_ref.shape)


def place(received, share):
    blocks, rows, lanes = received.shape
    groups = rows // share
    return pl.pallas_call(
        place_kernel,
        grid=(groups,),
        in_specs=[pl.BlockSpec((blocks, share, lanes), lambda g: (0, g, 0))],
        out_specs=pl.BlockSpec((4, lanes // 4, blocks * share), lambda g: (g, 0, 0)),
        out_shape=jax.ShapeDtypeStruct((groups * 4, lanes // 4, blocks * share), bf16),
        compiler_params=params(),
        name="place",
    )(received)


def exchange(blocks):
    return lax.all_to_all(blocks, everyone, split_axis=0, concat_axis=0, tiled=True)


def on_device(
    pair_rep,
    residue_mask,
    pair_mask,
    input_gain,
    input_bias,
    left_proj,
    left_gate,
    right_proj,
    right_gate,
    gate_weight,
    output_gain,
    output_bias,
    out_weight,
):
    rows = pair_rep.shape[0]
    parts = lax.axis_size("rep")
    share = rows // parts
    own = lax.axis_index("rep")
    where = jnp.stack([lax.axis_index("dap") * parts + own, own]).astype(jnp.int32)
    weights = jnp.stack([left_proj.T, left_gate.T, right_proj.T, right_gate.T, gate_weight.T])
    weights = lax.all_gather(weights, "rep", axis=0)
    normed = norm_in(where, pair_rep, input_gain, input_bias, share, 256)
    both = project(where, residue_mask, normed, weights, pair_mask, 256)
    both = exchange(both)
    gating = gates(normed, weights, 256)
    product = exchange(products(both, 32))
    update = updates(product, gating, output_gain, output_bias, out_weight.T)
    total, tile = product.shape[0], update.shape[-1]
    update = exchange(update.reshape(total, -1, tile))
    return jnp.swapaxes(place(update, share), 1, 2)


def solution(mesh):
    in_specs = (
        P("dap", None, None),
        P(),
        P("dap", None),
        P(),
        P(),
        P(None, "rep"),
        P(None, "rep"),
        P(None, "rep"),
        P(None, "rep"),
        P(None, "rep"),
        P(),
        P(),
        P(),
    )
    out_specs = P("rep", None, "dap")
    return jax.shard_map(
        on_device, mesh=mesh, in_specs=in_specs, out_specs=out_specs, check_vma=False
    )
```

```python
import jax
import jax.numpy as jnp
from jax import lax
from jax.experimental import pallas as pl
from jax.experimental.pallas import tpu as pltpu
from jax.sharding import PartitionSpec as P

eps = 1e-05
bf16 = jnp.bfloat16
f32 = jnp.float32
everyone = ("dap", "rep")
lane = 128
pack = 4


def params(mib):
    return pltpu.CompilerParams(vmem_limit_bytes=mib * 2**20)


def stay(array):
    return pltpu.with_memory_space_constraint(array, pltpu.HBM)


def rows_by_rows(a, b):
    return lax.dot_general(a, b, (((1,), (1,)), ((), ())), preferred_element_type=f32)


def column(row):
    return jnp.broadcast_to(row, (lane, lane)).T


def widen(column, tile):
    return column if tile == lane else jnp.concatenate([column] * (tile // lane), -1)


def centring(width):
    row = lax.broadcasted_iota(jnp.int32, (width, width), 0)
    at = lax.broadcasted_iota(jnp.int32, (width, width), 1)
    return ((row == at).astype(f32) - 1.0 / width).astype(bf16)


def normed_columns(x, gain, bias):
    width = x.shape[1]
    centred = rows_by_rows(centring(width), x)
    var = jnp.sum(centred * centred, axis=0, keepdims=True) * (1.0 / width)
    return (centred * lax.rsqrt(var + eps) * gain + bias).astype(bf16)


def project_kernel(
    where,
    residues,
    x_ref,
    left_proj,
    left_gate,
    right_proj,
    right_gate,
    gain_ref,
    bias_ref,
    keep_ref,
    mask_ref,
    out_ref,
    held,
):
    rows, tile, width = x_ref.shape
    hidden = out_ref.shape[0]
    step = rows + 1
    weights = jnp.concatenate(
        [left_proj[...], left_gate[...], right_proj[...], right_gate[...]], 0
    )
    lanes = mask_ref[...].astype(f32)
    gain = widen(column(gain_ref[...]), tile)
    bias = widen(column(bias_ref[...]), tile)
    first = where[0] * rows
    for i in range(rows):
        y = jnp.dot(weights, normed_columns(x_ref[i], gain, bias), preferred_element_type=f32)
        keep = keep_ref[i : i + 1, :].astype(f32) * lanes * residues[first + i].astype(f32)
        half = keep * 0.5
        for side in range(2):
            linear = y[2 * side * hidden : (2 * side + 1) * hidden]
            gate = y[(2 * side + 1) * hidden : (2 * side + 2) * hidden]
            result = (jnp.tanh(gate * 0.5) + 1.0) * (linear * half)
            for part in range(tile // lane):
                held[side, part, pl.ds(i, hidden, stride=step), :] = result[
                    :, part * lane : (part + 1) * lane
                ]
    for side in range(2):
        for part in range(tile // lane):
            for c in range(hidden):
                out_ref[c, side, :, part * lane : (part + 1) * lane] = held[
                    side, part, pl.ds(c * step, rows), :
                ].astype(bf16)


def project(where, residue_mask, pair_rep, weights, gain, bias, pair_mask, tile):
    rows, total, width = pair_rep.shape
    hidden = weights[0].shape[0]

    def fixed(t, *_):
        return (0, 0)

    return pl.pallas_call(
        project_kernel,
        grid_spec=pltpu.PrefetchScalarGridSpec(
            num_scalar_prefetch=2,
            grid=(total // tile,),
            in_specs=[
                pl.BlockSpec((rows, tile, width), lambda t, *_: (0, t, 0)),
                *[pl.BlockSpec((hidden, width), fixed)] * 4,
                *[pl.BlockSpec((1, width), fixed)] * 2,
                pl.BlockSpec((rows, tile), lambda t, *_: (0, t)),
                pl.BlockSpec((1, tile), lambda t, *_: (0, t)),
            ],
            out_specs=pl.BlockSpec((hidden, 2, rows, tile), lambda t, *_: (0, 0, 0, t)),
            scratch_shapes=[pltpu.VMEM((2, tile // lane, hidden * (rows + 1), lane), f32)],
        ),
        out_shape=pltpu.VMEM((hidden, 2, rows, total), bf16),
        compiler_params=params(32),
        name="project",
    )(
        where,
        residue_mask,
        stay(pair_rep),
        *[stay(w) for w in weights],
        stay(gain),
        stay(bias),
        stay(pair_mask),
        stay(residue_mask[None]),
    )


def gate_kernel(where, x_ref, w0, w1, w2, w3, gain_ref, bias_ref, out_ref, held):
    share, tile, _ = x_ref.shape
    channels = out_ref.shape[0]
    parts = (w0, w1, w2, w3)
    each = channels // len(parts)
    step = share + 1
    gain = widen(column(gain_ref[...]), tile)
    bias = widen(column(bias_ref[...]), tile)
    weights = jnp.concatenate([part[...] for part in parts], 0)
    for i in range(share):
        y = jnp.dot(weights, normed_columns(x_ref[i], gain, bias), preferred_element_type=f32)
        result = 0.5 * jnp.tanh(0.5 * y) + 0.5
        for shift in range(len(parts)):
            owner = lax.rem(where[1] - shift + len(parts), len(parts))
            for part in range(tile // lane):
                held[part, pl.ds(owner * (each * step) + i, each, stride=step), :] = result[
                    shift * each : (shift + 1) * each, part * lane : (part + 1) * lane
                ]
    for part in range(tile // lane):
        for c in range(channels):
            out_ref[c, :, part * lane : (part + 1) * lane] = held[
                part, pl.ds(c * step, share), :
            ].astype(bf16)


def gates(where, pair_rep, weights, gain, bias, share, tile):
    _, total, width = pair_rep.shape
    each = weights[0].shape[0]
    channels = each * len(weights)
    return pl.pallas_call(
        gate_kernel,
        grid_spec=pltpu.PrefetchScalarGridSpec(
            num_scalar_prefetch=1,
            grid=(total // tile,),
            in_specs=[
                pl.BlockSpec((share, tile, width), lambda t, where: (where[1], t, 0)),
                *[pl.BlockSpec((each, width), lambda t, where: (0, 0))] * len(weights),
                *[pl.BlockSpec((1, width), lambda t, where: (0, 0))] * 2,
            ],
            out_specs=pl.BlockSpec((channels, share, tile), lambda t, where: (0, 0, t)),
            scratch_shapes=[pltpu.VMEM((tile // lane, channels * (share + 1), lane), f32)],
        ),
        out_shape=pltpu.HBM((channels, share, total), bf16),
        compiler_params=params(16),
        cost_estimate=pl.CostEstimate(
            flops=2 * share * total * width * channels,
            bytes_accessed=4 * share * total * width,
            transcendentals=share * total * channels,
        ),
        name="gates",
    )(where, stay(pair_rep), *weights, stay(gain), stay(bias))


def product_kernel(left_ref, right_ref, out_ref):
    total = left_ref.shape[-1]
    left = left_ref[...].reshape(-1, total)
    right = right_ref[...].reshape(-1, total)
    out_ref[...] = rows_by_rows(left, right).astype(bf16).reshape(out_ref.shape)


def products(both, share, steps):
    blocks, _, rows, total = both.shape
    tile = blocks // steps
    return pl.pallas_call(
        product_kernel,
        grid=(steps,),
        in_specs=[
            pl.BlockSpec((tile, None, rows, total), lambda t: (t, 0, 0, 0)),
            pl.BlockSpec((blocks, None, rows, total), lambda t: (0, 1, 0, 0)),
        ],
        out_specs=pl.BlockSpec((tile * rows // share, share, total), lambda t: (t, 0, 0)),
        out_shape=jax.ShapeDtypeStruct((blocks * rows // share, share, total), bf16),
        compiler_params=params(20),
        name="products",
    )(both, both)


def update_kernel(p_ref, gate_ref, gain_ref, bias_ref, w_ref, out_ref, spread, gains, biases):
    hidden, share, tile = p_ref.shape
    channels = gate_ref.shape[0]
    span = lane // pack

    @pl.when(pl.program_id(0) == 0)
    def _():
        wide = (hidden, hidden * share)
        source = lax.broadcasted_iota(jnp.int32, wide, 0) * share
        target = lax.broadcasted_iota(jnp.int32, wide, 1)
        repeat = jnp.logical_and(target >= source, target < source + share)
        along = jnp.dot(w_ref[...], repeat.astype(bf16), preferred_element_type=f32)
        row = lax.broadcasted_iota(jnp.int32, (1, share, hidden * share), 1)
        place = lax.broadcasted_iota(jnp.int32, (1, share, hidden * share), 2)
        own = (lax.rem(place, share) == row).astype(f32)
        spread[...] = (along[:, None, :] * own).reshape(spread.shape).astype(bf16)
        gains[...] = jnp.broadcast_to(column(gain_ref[...])[:, None, :], gains.shape)
        biases[...] = jnp.broadcast_to(column(bias_ref[...])[:, None, :], biases.shape)

    values = p_ref[...].astype(f32)
    mean = jnp.sum(values, axis=0, keepdims=True) * (1.0 / hidden)
    centred = values - mean
    var = jnp.sum(centred * centred, axis=0, keepdims=True) * (1.0 / hidden)
    normed = centred * lax.rsqrt(var + eps) * widen(gains[...], tile) + widen(biases[...], tile)
    normed = normed.reshape(hidden * share, tile).astype(bf16)
    projected = jnp.dot(spread[...], normed, preferred_element_type=f32)
    gate = gate_ref[...].astype(f32).reshape(channels * share, tile)
    result = (gate * projected).reshape(channels // pack, pack, share, tile)
    for block in range(tile // span):
        first = block * span
        piece = jnp.concatenate(
            [result[:, c, :, first : first + span] for c in range(pack)], axis=-1
        )
        out_ref[block] = piece.astype(bf16).reshape(out_ref.shape[1:])


def updates(product, gating, gain, bias, weights, tile):
    hidden, share, total = product.shape
    channels = gating.shape[0]
    span = lane // pack
    rows = channels * share // pack
    return pl.pallas_call(
        update_kernel,
        grid=(total // tile,),
        in_specs=[
            pl.BlockSpec((hidden, share, tile), lambda t: (0, 0, t)),
            pl.BlockSpec((channels, share, tile), lambda t: (0, 0, t)),
            pl.BlockSpec((1, hidden), lambda t: (0, 0)),
            pl.BlockSpec((1, hidden), lambda t: (0, 0)),
            pl.BlockSpec((channels, hidden), lambda t: (0, 0)),
        ],
        out_specs=pl.BlockSpec((tile // span, rows, lane), lambda t: (t, 0, 0)),
        out_shape=jax.ShapeDtypeStruct((total // span, rows, lane), bf16),
        scratch_shapes=[
            pltpu.VMEM((channels * share, hidden * share), bf16),
            pltpu.VMEM((hidden, share, lane), f32),
            pltpu.VMEM((hidden, share, lane), f32),
        ],
        compiler_params=params(28),
        name="updates",
    )(product, stay(gating), stay(gain), stay(bias), weights)


def place_kernel(u_ref, out_ref):
    blocks, rows, lanes = u_ref.shape
    groups = out_ref.shape[0] // pack
    share = rows // groups
    for g in range(groups):
        flat = u_ref[:, g * share : (g + 1) * share, :].astype(f32).reshape(blocks * share, lanes)
        out_ref[pack * g : pack * (g + 1)] = flat.T.astype(bf16).reshape(
            pack, lanes // pack, blocks * share
        )


def place(received, share, each):
    blocks, rows, lanes = received.shape
    groups = rows // share
    shape = (lanes // pack, blocks * share)
    return pl.pallas_call(
        place_kernel,
        grid=(groups // each,),
        in_specs=[pl.BlockSpec((blocks, share * each, lanes), lambda g: (0, g, 0))],
        out_specs=pl.BlockSpec((pack * each, *shape), lambda g: (g, 0, 0)),
        out_shape=jax.ShapeDtypeStruct((groups * pack, *shape), bf16),
        compiler_params=params(20),
        name="place",
    )(received)


def exchange(blocks, axes):
    return lax.all_to_all(blocks, axes, split_axis=0, concat_axis=0, tiled=True)


def from_before(own, axis):
    count = lax.axis_size(axis)
    return [own] + [
        lax.ppermute(own, axis, [(k, (k + shift) % count) for k in range(count)])
        for shift in range(1, count)
    ]


def on_device(
    pair_rep,
    residue_mask,
    pair_mask,
    input_gain,
    input_bias,
    left_proj,
    left_gate,
    right_proj,
    right_gate,
    gate_weight,
    output_gain,
    output_bias,
    out_weight,
):
    rows, total, _ = pair_rep.shape
    parts = lax.axis_size("rep")
    share = rows // parts
    where = jnp.stack([lax.axis_index("dap"), lax.axis_index("rep")]).astype(jnp.int32)
    gain_in, bias_in = input_gain[None], input_bias[None]
    all_gates = from_before(gate_weight.T, "rep")
    both = project(
        where,
        residue_mask,
        pair_rep,
        [left_proj.T, left_gate.T, right_proj.T, right_gate.T],
        gain_in,
        bias_in,
        pair_mask,
        256,
    )
    both, all_gates = lax.optimization_barrier((both, all_gates))
    both = exchange(both, "dap")
    both, all_gates = lax.optimization_barrier((both, all_gates))
    gating = gates(where, pair_rep, all_gates, gain_in, bias_in, share, 256)

    def arrival(values):
        per = values.shape[0] // parts
        return jnp.swapaxes(values.reshape(parts, per, *values.shape[1:]), 0, 1).reshape(
            values.shape
        )

    product = exchange(products(both, share, 2), everyone)
    update = updates(
        product,
        gating,
        arrival(output_gain)[None],
        arrival(output_bias)[None],
        arrival(out_weight).T,
        256,
    )
    update = exchange(update.reshape(total // share, -1, lane), everyone)
    return jnp.swapaxes(place(update, share, 4), 1, 2)


def solution(mesh):
    in_specs = (
        P("dap", None, None),
        P(),
        P("dap", None),
        P(),
        P(),
        P(None, "rep"),
        P(None, "rep"),
        P(None, "rep"),
        P(None, "rep"),
        P(None, "rep"),
        P(),
        P(),
        P(),
    )
    out_specs = P("rep", None, "dap")
    return jax.shard_map(
        on_device, mesh=mesh, in_specs=in_specs, out_specs=out_specs, check_vma=False
    )
```

```python
import functools

import jax
import jax.numpy as jnp
from jax import lax
from jax.experimental import pallas as pl
from jax.experimental.pallas import tpu as pltpu
from jax.sharding import PartitionSpec as P

eps = 1e-05
bf16 = jnp.bfloat16
f32 = jnp.float32
everyone = ("dap", "rep")
lane = 128
pack = 4


def params(mib):
    return pltpu.CompilerParams(vmem_limit_bytes=mib * 2**20)


def stay(array):
    return pltpu.with_memory_space_constraint(array, pltpu.HBM)


def near(array):
    return pltpu.with_memory_space_constraint(array, pltpu.VMEM)


whole = pl.BlockSpec(memory_space=pltpu.VMEM)


def rows_by_rows(a, b):
    return lax.dot_general(a, b, (((1,), (1,)), ((), ())), preferred_element_type=f32)


def column(row):
    return jnp.broadcast_to(row, (lane, lane)).T


def widen(column, tile):
    return column if tile == lane else jnp.concatenate([column] * (tile // lane), -1)


def centring(width):
    row = lax.broadcasted_iota(jnp.int32, (width, width), 0)
    at = lax.broadcasted_iota(jnp.int32, (width, width), 1)
    return ((row == at).astype(f32) - 1.0 / width).astype(bf16)


def normed_columns(x, gain, bias):
    width = x.shape[1]
    centred = rows_by_rows(centring(width), x)
    var = jnp.sum(centred * centred, axis=0, keepdims=True) * (1.0 / width)
    return (centred * lax.rsqrt(var + eps) * gain + bias).astype(bf16)


def project_kernel(
    where,
    residues,
    x_ref,
    left_proj,
    left_gate,
    right_proj,
    right_gate,
    gain_ref,
    bias_ref,
    keep_ref,
    mask_ref,
    out_ref,
    held,
):
    rows, tile, width = x_ref.shape
    hidden = out_ref.shape[0]
    step = rows + 1
    begin = pl.program_id(0) * tile
    weights = jnp.concatenate(
        [left_proj[...], left_gate[...], right_proj[...], right_gate[...]], 0
    )
    lanes = mask_ref[...].astype(f32)
    gain = widen(column(gain_ref[...]), tile)
    bias = widen(column(bias_ref[...]), tile)
    first = where[0] * rows
    for i in range(rows):
        y = jnp.dot(weights, normed_columns(x_ref[i], gain, bias), preferred_element_type=f32)
        keep = keep_ref[i : i + 1, :].astype(f32) * lanes * residues[first + i].astype(f32)
        half = keep * 0.5
        for side in range(2):
            linear = y[2 * side * hidden : (2 * side + 1) * hidden]
            gate = y[(2 * side + 1) * hidden : (2 * side + 2) * hidden]
            result = (jnp.tanh(gate * 0.5) + 1.0) * (linear * half)
            for part in range(tile // lane):
                held[side, part, pl.ds(i, hidden, stride=step), :] = result[
                    :, part * lane : (part + 1) * lane
                ]
    for side in range(2):
        for part in range(tile // lane):
            for c in range(hidden):
                across = pl.ds(pl.multiple_of(begin + part * lane, lane), lane)
                out_ref[c, side, :, across] = held[side, part, pl.ds(c * step, rows), :].astype(
                    bf16
                )


def project(where, residue_mask, pair_rep, weights, gain, bias, pair_mask, tile):
    rows, total, width = pair_rep.shape
    hidden = weights[0].shape[0]

    def fixed(t, *_):
        return (0, 0)

    return pl.pallas_call(
        project_kernel,
        grid_spec=pltpu.PrefetchScalarGridSpec(
            num_scalar_prefetch=2,
            grid=(total // tile,),
            in_specs=[
                pl.BlockSpec((rows, tile, width), lambda t, *_: (0, t, 0)),
                *[pl.BlockSpec((hidden, width), fixed)] * 4,
                *[pl.BlockSpec((1, width), fixed)] * 2,
                pl.BlockSpec((rows, tile), lambda t, *_: (0, t)),
                pl.BlockSpec((1, tile), lambda t, *_: (0, t)),
            ],
            out_specs=whole,
            scratch_shapes=[pltpu.VMEM((2, tile // lane, hidden * (rows + 1), lane), f32)],
        ),
        out_shape=pltpu.VMEM((hidden, 2, rows, total), bf16),
        compiler_params=params(32),
        name="project",
    )(
        where,
        residue_mask,
        stay(pair_rep),
        *[stay(w) for w in weights],
        stay(gain),
        stay(bias),
        stay(pair_mask),
        stay(residue_mask[None]),
    )


def gate_kernel(where, x_ref, w0, w1, w2, w3, gain_ref, bias_ref, out_ref, held):
    share, tile, _ = x_ref.shape
    channels = out_ref.shape[0]
    parts = (w0, w1, w2, w3)
    each = channels // len(parts)
    step = share + 1
    gain = widen(column(gain_ref[...]), tile)
    bias = widen(column(bias_ref[...]), tile)
    weights = jnp.concatenate([part[...] for part in parts], 0)
    for i in range(share):
        y = jnp.dot(weights, normed_columns(x_ref[i], gain, bias), preferred_element_type=f32)
        result = 0.5 * jnp.tanh(0.5 * y) + 0.5
        for shift in range(len(parts)):
            owner = lax.rem(where[1] - shift + len(parts), len(parts))
            for part in range(tile // lane):
                held[part, pl.ds(owner * (each * step) + i, each, stride=step), :] = result[
                    shift * each : (shift + 1) * each, part * lane : (part + 1) * lane
                ]
    for part in range(tile // lane):
        for c in range(channels):
            out_ref[c, :, part * lane : (part + 1) * lane] = held[
                part, pl.ds(c * step, share), :
            ].astype(bf16)


def gates(where, pair_rep, weights, gain, bias, share, tile):
    _, total, width = pair_rep.shape
    each = weights[0].shape[0]
    channels = each * len(weights)
    return pl.pallas_call(
        gate_kernel,
        grid_spec=pltpu.PrefetchScalarGridSpec(
            num_scalar_prefetch=1,
            grid=(total // tile,),
            in_specs=[
                pl.BlockSpec((share, tile, width), lambda t, where: (where[1], t, 0)),
                *[pl.BlockSpec((each, width), lambda t, where: (0, 0))] * len(weights),
                *[pl.BlockSpec((1, width), lambda t, where: (0, 0))] * 2,
            ],
            out_specs=pl.BlockSpec((None, channels, share, tile), lambda t, where: (t, 0, 0, 0)),
            scratch_shapes=[pltpu.VMEM((tile // lane, channels * (share + 1), lane), f32)],
        ),
        out_shape=pltpu.HBM((total // tile, channels, share, tile), bf16),
        compiler_params=params(16),
        cost_estimate=pl.CostEstimate(
            flops=2 * share * total * width * channels,
            bytes_accessed=4 * share * total * width,
            transcendentals=share * total * channels,
        ),
        name="gates",
    )(where, stay(pair_rep), *weights, stay(gain), stay(bias))


def product_kernel(both_ref, out_ref):
    blocks, _, rows, total = both_ref.shape
    tile = out_ref.shape[0] * out_ref.shape[1] // rows
    left = both_ref[pl.ds(pl.program_id(0) * tile, tile), 0].reshape(-1, total)
    right = both_ref[:, 1].reshape(-1, total)
    out_ref[...] = rows_by_rows(left, right).astype(bf16).reshape(out_ref.shape)


def products(both, share, steps):
    blocks, _, rows, total = both.shape
    count = blocks * rows // share
    return pl.pallas_call(
        product_kernel,
        grid=(steps,),
        in_specs=[whole],
        out_specs=pl.BlockSpec((count // steps, share, total), lambda t: (t, 0, 0)),
        out_shape=pltpu.HBM((count, share, total), bf16),
        compiler_params=params(20),
        name="products",
    )(near(both))


def update_kernel(
    p_ref, gate_hbm, gain_ref, bias_ref, w_ref, out_ref, gate_ref, spread, gains, biases, sems, *, tile
):
    hidden, share, total = p_ref.shape
    channels = gate_ref.shape[1]
    span = lane // pack
    starts = range(0, total, tile)
    copies = [
        pltpu.make_async_copy(gate_hbm.at[number], gate_ref.at[number], sems.at[number])
        for number in range(len(starts))
    ]
    for copy in copies:
        copy.start()
    wide = (hidden, hidden * share)
    source = lax.broadcasted_iota(jnp.int32, wide, 0) * share
    target = lax.broadcasted_iota(jnp.int32, wide, 1)
    repeat = jnp.logical_and(target >= source, target < source + share)
    along = jnp.dot(w_ref[...], repeat.astype(bf16), preferred_element_type=f32)
    row = lax.broadcasted_iota(jnp.int32, (1, share, hidden * share), 1)
    place = lax.broadcasted_iota(jnp.int32, (1, share, hidden * share), 2)
    own = (lax.rem(place, share) == row).astype(f32)
    spread[...] = (along[:, None, :] * own).reshape(spread.shape).astype(bf16)
    gains[...] = jnp.broadcast_to(column(gain_ref[...])[:, None, :], gains.shape)
    biases[...] = jnp.broadcast_to(column(bias_ref[...])[:, None, :], biases.shape)
    for number, begin in enumerate(starts):
        across = slice(begin, begin + tile)
        values = p_ref[:, :, across].astype(f32)
        mean = jnp.sum(values, axis=0, keepdims=True) * (1.0 / hidden)
        centred = values - mean
        var = jnp.sum(centred * centred, axis=0, keepdims=True) * (1.0 / hidden)
        normed = centred * lax.rsqrt(var + eps) * widen(gains[...], tile) + widen(
            biases[...], tile
        )
        normed = normed.reshape(hidden * share, tile).astype(bf16)
        projected = jnp.dot(spread[...], normed, preferred_element_type=f32)
        if number == 0:
            for copy in copies:
                copy.wait()
        gate = gate_ref[number].astype(f32).reshape(channels * share, tile)
        result = (gate * projected).reshape(channels // pack, pack, share, tile)
        for first in range(0, tile, span):
            piece = jnp.concatenate(
                [result[:, c, :, first : first + span] for c in range(pack)], axis=-1
            )
            out_ref[(begin + first) // span] = piece.astype(bf16).reshape(out_ref.shape[1:])


def updates(product, gating, gain, bias, weights, tile):
    hidden, share, total = product.shape
    channels = gating.shape[1]
    span = lane // pack
    return pl.pallas_call(
        functools.partial(update_kernel, tile=tile),
        in_specs=[whole, pl.BlockSpec(memory_space=pltpu.HBM), whole, whole, whole],
        out_specs=whole,
        out_shape=pltpu.VMEM((total // span, channels * share // pack, lane), bf16),
        scratch_shapes=[
            pltpu.VMEM(gating.shape, bf16),
            pltpu.VMEM((channels * share, hidden * share), bf16),
            pltpu.VMEM((hidden, share, lane), f32),
            pltpu.VMEM((hidden, share, lane), f32),
            pltpu.SemaphoreType.DMA((total // tile,)),
        ],
        compiler_params=params(28),
        name="updates",
    )(near(product), stay(gating), gain, bias, weights)


def place_kernel(u_ref, out_ref):
    blocks, rows, lanes = u_ref.shape
    groups = out_ref.shape[0] // pack
    share = rows // groups
    for g in range(groups):
        flat = u_ref[:, g * share : (g + 1) * share, :].astype(f32).reshape(blocks * share, lanes)
        out_ref[pack * g : pack * (g + 1)] = flat.T.astype(bf16).reshape(
            pack, lanes // pack, blocks * share
        )


def place(received, share, each):
    blocks, rows, lanes = received.shape
    groups = rows // share
    shape = (lanes // pack, blocks * share)
    return pl.pallas_call(
        place_kernel,
        grid=(groups // each,),
        in_specs=[pl.BlockSpec((blocks, share * each, lanes), lambda g: (0, g, 0))],
        out_specs=pl.BlockSpec((pack * each, *shape), lambda g: (g, 0, 0)),
        out_shape=jax.ShapeDtypeStruct((groups * pack, *shape), bf16),
        compiler_params=params(20),
        name="place",
    )(received)


def exchange(blocks, axes):
    return lax.all_to_all(blocks, axes, split_axis=0, concat_axis=0, tiled=True)


def from_before(own, axis):
    count = lax.axis_size(axis)
    parts = [
        lax.ppermute(own, axis, [(k, (k + shift) % count) for k in range(count)])
        for shift in range(count - 1, 0, -1)
    ]
    return [own] + parts[::-1]


def on_device(
    pair_rep,
    residue_mask,
    pair_mask,
    input_gain,
    input_bias,
    left_proj,
    left_gate,
    right_proj,
    right_gate,
    gate_weight,
    output_gain,
    output_bias,
    out_weight,
):
    rows, total, _ = pair_rep.shape
    parts = lax.axis_size("rep")
    share = rows // parts
    where = jnp.stack([lax.axis_index("dap"), lax.axis_index("rep")]).astype(jnp.int32)
    gain_in, bias_in = input_gain[None], input_bias[None]
    all_gates = from_before(gate_weight.T, "rep")
    both = project(
        where,
        residue_mask,
        pair_rep,
        [left_proj.T, left_gate.T, right_proj.T, right_gate.T],
        gain_in,
        bias_in,
        pair_mask,
        256,
    )
    both, all_gates = lax.optimization_barrier((both, all_gates))
    both = exchange(both, "dap")
    both, all_gates, out_weight = lax.optimization_barrier((both, all_gates, out_weight))
    gating = gates(where, pair_rep, all_gates, gain_in, bias_in, share, 256)

    def arrival(values):
        per = values.shape[0] // parts
        return jnp.swapaxes(values.reshape(parts, per, *values.shape[1:]), 0, 1).reshape(
            values.shape
        )

    product = exchange(products(both, share, 2), everyone)
    update = updates(
        product,
        gating,
        arrival(output_gain)[None],
        arrival(output_bias)[None],
        arrival(out_weight).T,
        256,
    )
    update = exchange(update.reshape(total // share, -1, lane), everyone)
    return jnp.swapaxes(place(update, share, 4), 1, 2)


def solution(mesh):
    in_specs = (
        P("dap", None, None),
        P(),
        P("dap", None),
        P(),
        P(),
        P(None, "rep"),
        P(None, "rep"),
        P(None, "rep"),
        P(None, "rep"),
        P(None, "rep"),
        P(),
        P(),
        P(),
    )
    out_specs = P("rep", None, "dap")
    return jax.shard_map(
        on_device, mesh=mesh, in_specs=in_specs, out_specs=out_specs, check_vma=False
    )
```

```python
import functools

import jax
import jax.numpy as jnp
from jax import lax
from jax.experimental import pallas as pl
from jax.experimental.pallas import tpu as pltpu
from jax.sharding import PartitionSpec as P

eps = 1e-05
bf16 = jnp.bfloat16
f32 = jnp.float32
everyone = ("dap", "rep")
lane = 128
pack = 4


def params(mib):
    return pltpu.CompilerParams(vmem_limit_bytes=mib * 2**20)


def stay(array):
    return pltpu.with_memory_space_constraint(array, pltpu.HBM)


def near(array):
    return pltpu.with_memory_space_constraint(array, pltpu.VMEM)


whole = pl.BlockSpec(memory_space=pltpu.VMEM)


def rows_by_rows(a, b):
    return lax.dot_general(a, b, (((1,), (1,)), ((), ())), preferred_element_type=f32)


def column(row):
    return jnp.broadcast_to(row, (lane, lane)).T


def widen(column, tile):
    return column if tile == lane else jnp.concatenate([column] * (tile // lane), -1)


def centring(width):
    row = lax.broadcasted_iota(jnp.int32, (width, width), 0)
    at = lax.broadcasted_iota(jnp.int32, (width, width), 1)
    return ((row == at).astype(f32) - 1.0 / width).astype(bf16)


def normed_columns(x, gain, bias):
    width = x.shape[1]
    centred = rows_by_rows(centring(width), x)
    var = jnp.sum(centred * centred, axis=0, keepdims=True) * (1.0 / width)
    return (centred * lax.rsqrt(var + eps) * gain + bias).astype(bf16)


def project_kernel(
    where,
    residues,
    x_ref,
    left_proj,
    left_gate,
    right_proj,
    right_gate,
    gain_ref,
    bias_ref,
    keep_ref,
    mask_ref,
    out_ref,
    held,
):
    rows, tile, width = x_ref.shape
    hidden = out_ref.shape[0]
    step = rows + 1
    begin = pl.program_id(0) * tile
    weights = jnp.concatenate(
        [left_proj[...], left_gate[...], right_proj[...], right_gate[...]], 0
    )
    lanes = mask_ref[...].astype(f32)
    gain = widen(column(gain_ref[...]), tile)
    bias = widen(column(bias_ref[...]), tile)
    first = where[0] * rows
    for i in range(rows):
        y = jnp.dot(weights, normed_columns(x_ref[i], gain, bias), preferred_element_type=f32)
        keep = keep_ref[i : i + 1, :].astype(f32) * lanes * residues[first + i].astype(f32)
        half = keep * 0.5
        for side in range(2):
            linear = y[2 * side * hidden : (2 * side + 1) * hidden]
            gate = y[(2 * side + 1) * hidden : (2 * side + 2) * hidden]
            result = (jnp.tanh(gate * 0.5) + 1.0) * (linear * half)
            for part in range(tile // lane):
                held[side, part, pl.ds(i, hidden, stride=step), :] = result[
                    :, part * lane : (part + 1) * lane
                ]
    for side in range(2):
        for part in range(tile // lane):
            for c in range(hidden):
                across = pl.ds(pl.multiple_of(begin + part * lane, lane), lane)
                out_ref[c, side, :, across] = held[side, part, pl.ds(c * step, rows), :].astype(
                    bf16
                )


def project(where, residue_mask, pair_rep, weights, gain, bias, pair_mask, tile):
    rows, total, width = pair_rep.shape
    hidden = weights[0].shape[0]

    def fixed(t, *_):
        return (0, 0)

    return pl.pallas_call(
        project_kernel,
        grid_spec=pltpu.PrefetchScalarGridSpec(
            num_scalar_prefetch=2,
            grid=(total // tile,),
            in_specs=[
                pl.BlockSpec((rows, tile, width), lambda t, *_: (0, t, 0)),
                *[pl.BlockSpec((hidden, width), fixed)] * 4,
                *[pl.BlockSpec((1, width), fixed)] * 2,
                pl.BlockSpec((rows, tile), lambda t, *_: (0, t)),
                pl.BlockSpec((1, tile), lambda t, *_: (0, t)),
            ],
            out_specs=whole,
            scratch_shapes=[pltpu.VMEM((2, tile // lane, hidden * (rows + 1), lane), f32)],
        ),
        out_shape=pltpu.VMEM((hidden, 2, rows, total), bf16),
        compiler_params=params(32),
        name="project",
    )(
        where,
        residue_mask,
        stay(pair_rep),
        *[stay(w) for w in weights],
        stay(gain),
        stay(bias),
        stay(pair_mask),
        stay(residue_mask[None]),
    )


def gate_kernel(where, x_ref, w0, w1, w2, w3, gain_ref, bias_ref, out_ref, held):
    share, tile, _ = x_ref.shape
    channels = out_ref.shape[0]
    parts = (w0, w1, w2, w3)
    each = channels // len(parts)
    step = share + 1
    gain = widen(column(gain_ref[...]), tile)
    bias = widen(column(bias_ref[...]), tile)
    weights = jnp.concatenate([part[...] for part in parts], 0)
    for i in range(share):
        y = jnp.dot(weights, normed_columns(x_ref[i], gain, bias), preferred_element_type=f32)
        result = 0.5 * jnp.tanh(0.5 * y) + 0.5
        for shift in range(len(parts)):
            owner = lax.rem(where[1] - shift + len(parts), len(parts))
            for part in range(tile // lane):
                held[part, pl.ds(owner * (each * step) + i, each, stride=step), :] = result[
                    shift * each : (shift + 1) * each, part * lane : (part + 1) * lane
                ]
    for part in range(tile // lane):
        for c in range(channels):
            out_ref[c, :, part * lane : (part + 1) * lane] = held[
                part, pl.ds(c * step, share), :
            ].astype(bf16)


def gates(where, pair_rep, weights, gain, bias, share, tile):
    _, total, width = pair_rep.shape
    each = weights[0].shape[0]
    channels = each * len(weights)
    return pl.pallas_call(
        gate_kernel,
        grid_spec=pltpu.PrefetchScalarGridSpec(
            num_scalar_prefetch=1,
            grid=(total // tile,),
            in_specs=[
                pl.BlockSpec((share, tile, width), lambda t, where: (where[1], t, 0)),
                *[pl.BlockSpec((each, width), lambda t, where: (0, 0))] * len(weights),
                *[pl.BlockSpec((1, width), lambda t, where: (0, 0))] * 2,
            ],
            out_specs=pl.BlockSpec((None, channels, share, tile), lambda t, where: (t, 0, 0, 0)),
            scratch_shapes=[pltpu.VMEM((tile // lane, channels * (share + 1), lane), f32)],
        ),
        out_shape=pltpu.HBM((total // tile, channels, share, tile), bf16),
        compiler_params=params(16),
        cost_estimate=pl.CostEstimate(
            flops=2 * share * total * width * channels,
            bytes_accessed=4 * share * total * width,
            transcendentals=share * total * channels,
        ),
        name="gates",
    )(where, stay(pair_rep), *weights, stay(gain), stay(bias))


def product_kernel(both_ref, out_hbm, out_ref, sems, *, counts):
    blocks, _, rows, total = both_ref.shape
    share = out_ref.shape[1]
    copies, begin = [], 0
    for number, count in enumerate(counts):
        left = both_ref[begin : begin + count, 0].reshape(-1, total)
        right = both_ref[:, 1].reshape(-1, total)
        at = pl.ds(begin * rows // share, count * rows // share)
        out_ref[at] = rows_by_rows(left, right).astype(bf16).reshape(-1, share, total)
        copies.append(pltpu.make_async_copy(out_ref.at[at], out_hbm.at[at], sems.at[number]))
        copies[-1].start()
        begin += count
    for copy in copies:
        copy.wait()


def products(both, share, counts):
    blocks, _, rows, total = both.shape
    shape = (blocks * rows // share, share, total)
    return pl.pallas_call(
        functools.partial(product_kernel, counts=counts),
        in_specs=[whole],
        out_specs=pl.BlockSpec(memory_space=pltpu.HBM),
        out_shape=pltpu.HBM(shape, bf16),
        scratch_shapes=[pltpu.VMEM(shape, bf16), pltpu.SemaphoreType.DMA((len(counts),))],
        compiler_params=params(20),
        name="products",
    )(near(both))


def update_kernel(
    p_ref, gate_hbm, gain_ref, bias_ref, w_ref, out_ref, gate_ref, spread, gains, biases, sems, *, tile
):
    hidden, share, total = p_ref.shape
    channels = gate_ref.shape[1]
    span = lane // pack
    starts = range(0, total, tile)
    copies = [
        pltpu.make_async_copy(gate_hbm.at[number], gate_ref.at[number], sems.at[number])
        for number in range(len(starts))
    ]
    for copy in copies:
        copy.start()
    wide = (hidden, hidden * share)
    source = lax.broadcasted_iota(jnp.int32, wide, 0) * share
    target = lax.broadcasted_iota(jnp.int32, wide, 1)
    repeat = jnp.logical_and(target >= source, target < source + share)
    along = jnp.dot(w_ref[...], repeat.astype(bf16), preferred_element_type=f32)
    row = lax.broadcasted_iota(jnp.int32, (1, share, hidden * share), 1)
    place = lax.broadcasted_iota(jnp.int32, (1, share, hidden * share), 2)
    own = (lax.rem(place, share) == row).astype(f32)
    spread[...] = (along[:, None, :] * own).reshape(spread.shape).astype(bf16)
    gains[...] = jnp.broadcast_to(column(gain_ref[...])[:, None, :], gains.shape)
    biases[...] = jnp.broadcast_to(column(bias_ref[...])[:, None, :], biases.shape)

    def project_tile(begin):
        values = p_ref[:, :, begin : begin + tile].astype(f32)
        mean = jnp.sum(values, axis=0, keepdims=True) * (1.0 / hidden)
        centred = values - mean
        var = jnp.sum(centred * centred, axis=0, keepdims=True) * (1.0 / hidden)
        normed = centred * lax.rsqrt(var + eps) * widen(gains[...], tile) + widen(
            biases[...], tile
        )
        normed = normed.reshape(hidden * share, tile).astype(bf16)
        return jnp.dot(spread[...], normed, preferred_element_type=f32)

    def gate_tile(number, projected):
        gate = gate_ref[number].astype(f32).reshape(channels * share, tile)
        result = (gate * projected).reshape(channels // pack, pack, share, tile)
        for first in range(0, tile, span):
            piece = jnp.concatenate(
                [result[:, c, :, first : first + span] for c in range(pack)], axis=-1
            )
            out_ref[(starts[number] + first) // span] = piece.astype(bf16).reshape(
                out_ref.shape[1:]
            )

    ahead = min(2, len(starts))
    early = [project_tile(starts[number]) for number in range(ahead)]
    for copy in copies:
        copy.wait()
    for number in range(len(starts)):
        gate_tile(number, early[number] if number < ahead else project_tile(starts[number]))


def updates(product, gating, gain, bias, weights, tile):
    hidden, share, total = product.shape
    channels = gating.shape[1]
    span = lane // pack
    return pl.pallas_call(
        functools.partial(update_kernel, tile=tile),
        in_specs=[whole, pl.BlockSpec(memory_space=pltpu.HBM), whole, whole, whole],
        out_specs=whole,
        out_shape=pltpu.VMEM((total // span, channels * share // pack, lane), bf16),
        scratch_shapes=[
            pltpu.VMEM(gating.shape, bf16),
            pltpu.VMEM((channels * share, hidden * share), bf16),
            pltpu.VMEM((hidden, share, lane), f32),
            pltpu.VMEM((hidden, share, lane), f32),
            pltpu.SemaphoreType.DMA((total // tile,)),
        ],
        compiler_params=params(28),
        name="updates",
    )(near(product), stay(gating), gain, bias, weights)


def place_kernel(u_ref, out_ref):
    blocks, rows, lanes = u_ref.shape
    groups = out_ref.shape[0] // pack
    share = rows // groups
    for g in range(groups):
        flat = u_ref[:, g * share : (g + 1) * share, :].astype(f32).reshape(blocks * share, lanes)
        out_ref[pack * g : pack * (g + 1)] = flat.T.astype(bf16).reshape(
            pack, lanes // pack, blocks * share
        )


def place(received, share, each):
    blocks, rows, lanes = received.shape
    groups = rows // share
    shape = (lanes // pack, blocks * share)
    return pl.pallas_call(
        place_kernel,
        grid=(groups // each,),
        in_specs=[pl.BlockSpec((blocks, share * each, lanes), lambda g: (0, g, 0))],
        out_specs=pl.BlockSpec((pack * each, *shape), lambda g: (g, 0, 0)),
        out_shape=jax.ShapeDtypeStruct((groups * pack, *shape), bf16),
        compiler_params=params(20),
        name="place",
    )(received)


def exchange(blocks, axes):
    return lax.all_to_all(blocks, axes, split_axis=0, concat_axis=0, tiled=True)


def from_before(own, axis):
    count = lax.axis_size(axis)
    parts = [
        lax.ppermute(own, axis, [(k, (k + shift) % count) for k in range(count)])
        for shift in range(count - 1, 0, -1)
    ]
    return [own] + parts[::-1]


def on_device(
    pair_rep,
    residue_mask,
    pair_mask,
    input_gain,
    input_bias,
    left_proj,
    left_gate,
    right_proj,
    right_gate,
    gate_weight,
    output_gain,
    output_bias,
    out_weight,
):
    rows, total, _ = pair_rep.shape
    parts = lax.axis_size("rep")
    share = rows // parts
    where = jnp.stack([lax.axis_index("dap"), lax.axis_index("rep")]).astype(jnp.int32)
    gain_in, bias_in = input_gain[None], input_bias[None]
    all_gates = from_before(gate_weight.T, "rep")
    both = project(
        where,
        residue_mask,
        pair_rep,
        [left_proj.T, left_gate.T, right_proj.T, right_gate.T],
        gain_in,
        bias_in,
        pair_mask,
        256,
    )
    both, all_gates = lax.optimization_barrier((both, all_gates))
    both = exchange(both, "dap")
    both, all_gates, out_weight = lax.optimization_barrier((both, all_gates, out_weight))
    gating = gates(where, pair_rep, all_gates, gain_in, bias_in, share, 256)

    def arrival(values):
        per = values.shape[0] // parts
        return jnp.swapaxes(values.reshape(parts, per, *values.shape[1:]), 0, 1).reshape(
            values.shape
        )

    product = exchange(products(both, share, (24, 8)), everyone)
    update = updates(
        product,
        gating,
        arrival(output_gain)[None],
        arrival(output_bias)[None],
        arrival(out_weight).T,
        256,
    )
    update = exchange(update.reshape(total // share, -1, lane), everyone)
    return jnp.swapaxes(place(update, share, 4), 1, 2)


def solution(mesh):
    in_specs = (
        P("dap", None, None),
        P(),
        P("dap", None),
        P(),
        P(),
        P(None, "rep"),
        P(None, "rep"),
        P(None, "rep"),
        P(None, "rep"),
        P(None, "rep"),
        P(),
        P(),
        P(),
    )
    out_specs = P("rep", None, "dap")
    return jax.shard_map(
        on_device, mesh=mesh, in_specs=in_specs, out_specs=out_specs, check_vma=False
    )
```

```python
import functools

import jax
import jax.numpy as jnp
from jax import lax
from jax.experimental import pallas as pl
from jax.experimental.pallas import tpu as pltpu
from jax.sharding import PartitionSpec as P

eps = 1e-05
bf16 = jnp.bfloat16
f32 = jnp.float32
everyone = ("dap", "rep")
lane = 128
pack = 4


def params(mib):
    return pltpu.CompilerParams(vmem_limit_bytes=mib * 2**20)


def stay(array):
    return pltpu.with_memory_space_constraint(array, pltpu.HBM)


def near(array):
    return pltpu.with_memory_space_constraint(array, pltpu.VMEM)


whole = pl.BlockSpec(memory_space=pltpu.VMEM)


def rows_by_rows(a, b):
    return lax.dot_general(a, b, (((1,), (1,)), ((), ())), preferred_element_type=f32)


def column(row):
    return jnp.broadcast_to(row, (lane, lane)).T


def widen(column, tile):
    return column if tile == lane else jnp.concatenate([column] * (tile // lane), -1)


def centring(width):
    row = lax.broadcasted_iota(jnp.int32, (width, width), 0)
    at = lax.broadcasted_iota(jnp.int32, (width, width), 1)
    return ((row == at).astype(f32) - 1.0 / width).astype(bf16)


def normed_columns(x, gain, bias):
    width = x.shape[1]
    centred = rows_by_rows(centring(width), x)
    var = jnp.sum(centred * centred, axis=0, keepdims=True) * (1.0 / width)
    return (centred * lax.rsqrt(var + eps) * gain + bias).astype(bf16)


def project_kernel(
    where,
    residues,
    x_ref,
    left_proj,
    left_gate,
    right_proj,
    right_gate,
    gain_ref,
    bias_ref,
    keep_ref,
    mask_ref,
    out_ref,
    held,
):
    rows, tile, width = x_ref.shape
    hidden = out_ref.shape[0]
    step = rows + 1
    begin = pl.program_id(0) * tile
    weights = jnp.concatenate(
        [left_proj[...], left_gate[...], right_proj[...], right_gate[...]], 0
    )
    lanes = mask_ref[...].astype(f32)
    gain = widen(column(gain_ref[...]), tile)
    bias = widen(column(bias_ref[...]), tile)
    first = where[0] * rows
    for i in range(rows):
        y = jnp.dot(weights, normed_columns(x_ref[i], gain, bias), preferred_element_type=f32)
        keep = keep_ref[i : i + 1, :].astype(f32) * lanes * residues[first + i].astype(f32)
        half = keep * 0.5
        for side in range(2):
            linear = y[2 * side * hidden : (2 * side + 1) * hidden]
            gate = y[(2 * side + 1) * hidden : (2 * side + 2) * hidden]
            result = (jnp.tanh(gate * 0.5) + 1.0) * (linear * half)
            for part in range(tile // lane):
                held[side, part, pl.ds(i, hidden, stride=step), :] = result[
                    :, part * lane : (part + 1) * lane
                ]
    for side in range(2):
        for part in range(tile // lane):
            for c in range(hidden):
                across = pl.ds(pl.multiple_of(begin + part * lane, lane), lane)
                out_ref[c, side, :, across] = held[side, part, pl.ds(c * step, rows), :].astype(
                    bf16
                )


def project(where, residue_mask, pair_rep, weights, gain, bias, pair_mask, tile):
    rows, total, width = pair_rep.shape
    hidden = weights[0].shape[0]

    def fixed(t, *_):
        return (0, 0)

    return pl.pallas_call(
        project_kernel,
        grid_spec=pltpu.PrefetchScalarGridSpec(
            num_scalar_prefetch=2,
            grid=(total // tile,),
            in_specs=[
                pl.BlockSpec((rows, tile, width), lambda t, *_: (0, t, 0)),
                *[pl.BlockSpec((hidden, width), fixed)] * 4,
                *[pl.BlockSpec((1, width), fixed)] * 2,
                pl.BlockSpec((rows, tile), lambda t, *_: (0, t)),
                pl.BlockSpec((1, tile), lambda t, *_: (0, t)),
            ],
            out_specs=whole,
            scratch_shapes=[pltpu.VMEM((2, tile // lane, hidden * (rows + 1), lane), f32)],
        ),
        out_shape=pltpu.VMEM((hidden, 2, rows, total), bf16),
        compiler_params=params(32),
        name="project",
    )(
        where,
        residue_mask,
        stay(pair_rep),
        *[stay(w) for w in weights],
        stay(gain),
        stay(bias),
        stay(pair_mask),
        stay(residue_mask[None]),
    )


def gate_kernel(where, x_ref, w0, w1, w2, w3, gain_ref, bias_ref, out_ref, held):
    share, tile, _ = x_ref.shape
    channels = out_ref.shape[0]
    parts = (w0, w1, w2, w3)
    each = channels // len(parts)
    step = share + 1
    gain = widen(column(gain_ref[...]), tile)
    bias = widen(column(bias_ref[...]), tile)
    weights = jnp.concatenate([part[...] for part in parts], 0)
    for i in range(share):
        y = jnp.dot(weights, normed_columns(x_ref[i], gain, bias), preferred_element_type=f32)
        result = 0.5 * jnp.tanh(0.5 * y) + 0.5
        for shift in range(len(parts)):
            high, low = lax.div(where[1], 2), lax.rem(where[1], 2)
            owner = 2 * (1 - high if shift & 2 else high) + (1 - low if shift & 1 else low)
            for part in range(tile // lane):
                held[part, pl.ds(owner * (each * step) + i, each, stride=step), :] = result[
                    shift * each : (shift + 1) * each, part * lane : (part + 1) * lane
                ]
    for part in range(tile // lane):
        for c in range(channels):
            out_ref[c, :, part * lane : (part + 1) * lane] = held[
                part, pl.ds(c * step, share), :
            ].astype(bf16)


def gates(where, pair_rep, weights, gain, bias, share, tile):
    _, total, width = pair_rep.shape
    each = weights[0].shape[0]
    channels = each * len(weights)
    return pl.pallas_call(
        gate_kernel,
        grid_spec=pltpu.PrefetchScalarGridSpec(
            num_scalar_prefetch=1,
            grid=(total // tile,),
            in_specs=[
                pl.BlockSpec((share, tile, width), lambda t, where: (where[1], t, 0)),
                *[pl.BlockSpec((each, width), lambda t, where: (0, 0))] * len(weights),
                *[pl.BlockSpec((1, width), lambda t, where: (0, 0))] * 2,
            ],
            out_specs=pl.BlockSpec((None, channels, share, tile), lambda t, where: (t, 0, 0, 0)),
            scratch_shapes=[pltpu.VMEM((tile // lane, channels * (share + 1), lane), f32)],
        ),
        out_shape=pltpu.HBM((total // tile, channels, share, tile), bf16),
        compiler_params=params(16),
        cost_estimate=pl.CostEstimate(
            flops=2 * share * total * width * channels,
            bytes_accessed=4 * share * total * width,
            transcendentals=share * total * channels,
        ),
        name="gates",
    )(where, stay(pair_rep), *weights, stay(gain), stay(bias))


def product_kernel(both_ref, out_hbm, out_ref, sems, *, counts):
    blocks, _, rows, total = both_ref.shape
    share = out_ref.shape[1]
    copies, begin = [], 0
    for number, count in enumerate(counts):
        left = both_ref[begin : begin + count, 0].reshape(-1, total)
        right = both_ref[:, 1].reshape(-1, total)
        at = pl.ds(begin * rows // share, count * rows // share)
        out_ref[at] = rows_by_rows(left, right).astype(bf16).reshape(-1, share, total)
        copies.append(pltpu.make_async_copy(out_ref.at[at], out_hbm.at[at], sems.at[number]))
        copies[-1].start()
        begin += count
    for copy in copies:
        copy.wait()


def products(both, share, counts):
    blocks, _, rows, total = both.shape
    shape = (blocks * rows // share, share, total)
    return pl.pallas_call(
        functools.partial(product_kernel, counts=counts),
        in_specs=[whole],
        out_specs=pl.BlockSpec(memory_space=pltpu.HBM),
        out_shape=pltpu.HBM(shape, bf16),
        scratch_shapes=[pltpu.VMEM(shape, bf16), pltpu.SemaphoreType.DMA((len(counts),))],
        compiler_params=params(20),
        name="products",
    )(near(both))


def update_kernel(
    p_ref, gate_hbm, gain_ref, bias_ref, w_ref, out_ref, gate_ref, spread, gains, biases, sems, *, tile
):
    hidden, share, total = p_ref.shape
    channels = gate_ref.shape[1]
    span = lane // pack
    starts = range(0, total, tile)
    copies = [
        pltpu.make_async_copy(gate_hbm.at[number], gate_ref.at[number], sems.at[number])
        for number in range(len(starts))
    ]
    for copy in copies:
        copy.start()
    wide = (hidden, hidden * share)
    source = lax.broadcasted_iota(jnp.int32, wide, 0) * share
    target = lax.broadcasted_iota(jnp.int32, wide, 1)
    repeat = jnp.logical_and(target >= source, target < source + share)
    along = jnp.dot(w_ref[...], repeat.astype(bf16), preferred_element_type=f32)
    row = lax.broadcasted_iota(jnp.int32, (1, share, hidden * share), 1)
    place = lax.broadcasted_iota(jnp.int32, (1, share, hidden * share), 2)
    own = (lax.rem(place, share) == row).astype(f32)
    spread[...] = (along[:, None, :] * own).reshape(spread.shape).astype(bf16)
    gains[...] = jnp.broadcast_to(column(gain_ref[...])[:, None, :], gains.shape)
    biases[...] = jnp.broadcast_to(column(bias_ref[...])[:, None, :], biases.shape)

    def project_tile(begin):
        values = p_ref[:, :, begin : begin + tile].astype(f32)
        mean = jnp.sum(values, axis=0, keepdims=True) * (1.0 / hidden)
        centred = values - mean
        var = jnp.sum(centred * centred, axis=0, keepdims=True) * (1.0 / hidden)
        normed = centred * lax.rsqrt(var + eps) * widen(gains[...], tile) + widen(
            biases[...], tile
        )
        normed = normed.reshape(hidden * share, tile).astype(bf16)
        return jnp.dot(spread[...], normed, preferred_element_type=f32)

    def gate_tile(number, projected):
        gate = gate_ref[number].astype(f32).reshape(channels * share, tile)
        result = (gate * projected).reshape(channels // pack, pack, share, tile)
        for first in range(0, tile, span):
            piece = jnp.concatenate(
                [result[:, c, :, first : first + span] for c in range(pack)], axis=-1
            )
            out_ref[(starts[number] + first) // span] = piece.astype(bf16).reshape(
                out_ref.shape[1:]
            )

    ahead = min(2, len(starts))
    early = [project_tile(starts[number]) for number in range(ahead)]
    for copy in copies:
        copy.wait()
    for number in range(len(starts)):
        gate_tile(number, early[number] if number < ahead else project_tile(starts[number]))


def updates(product, gating, gain, bias, weights, tile):
    hidden, share, total = product.shape
    channels = gating.shape[1]
    span = lane // pack
    return pl.pallas_call(
        functools.partial(update_kernel, tile=tile),
        in_specs=[whole, pl.BlockSpec(memory_space=pltpu.HBM), whole, whole, whole],
        out_specs=whole,
        out_shape=pltpu.VMEM((total // span, channels * share // pack, lane), bf16),
        scratch_shapes=[
            pltpu.VMEM(gating.shape, bf16),
            pltpu.VMEM((channels * share, hidden * share), bf16),
            pltpu.VMEM((hidden, share, lane), f32),
            pltpu.VMEM((hidden, share, lane), f32),
            pltpu.SemaphoreType.DMA((total // tile,)),
        ],
        compiler_params=params(28),
        name="updates",
    )(near(product), stay(gating), gain, bias, weights)


def place_kernel(u_ref, out_hbm, out_ref, sems, *, share):
    blocks, rows, lanes = u_ref.shape
    copies = []
    for g in range(rows // share):
        flat = u_ref[:, g * share : (g + 1) * share, :].astype(f32).reshape(blocks * share, lanes)
        at = pl.ds(g * pack, pack)
        out_ref[at] = flat.T.astype(bf16).reshape(pack, lanes // pack, blocks * share)
        copies.append(pltpu.make_async_copy(out_ref.at[at], out_hbm.at[at], sems.at[g]))
        copies[-1].start()
    for copy in copies:
        copy.wait()


def place(received, share):
    blocks, rows, lanes = received.shape
    shape = (rows // share * pack, lanes // pack, blocks * share)
    return pl.pallas_call(
        functools.partial(place_kernel, share=share),
        in_specs=[whole],
        out_specs=pl.BlockSpec(memory_space=pltpu.HBM),
        out_shape=pltpu.HBM(shape, bf16),
        scratch_shapes=[pltpu.VMEM(shape, bf16), pltpu.SemaphoreType.DMA((rows // share,))],
        compiler_params=params(20),
        name="place",
    )(near(received))


def exchange(blocks, axes):
    return lax.all_to_all(blocks, axes, split_axis=0, concat_axis=0, tiled=True)


def from_peers(own):
    return [own] + [
        lax.ppermute(own, "rep", [(k, k ^ distance) for k in range(4)]) for distance in (1, 2, 3)
    ]


def on_device(
    pair_rep,
    residue_mask,
    pair_mask,
    input_gain,
    input_bias,
    left_proj,
    left_gate,
    right_proj,
    right_gate,
    gate_weight,
    output_gain,
    output_bias,
    out_weight,
):
    rows, total, _ = pair_rep.shape
    parts = lax.axis_size("rep")
    share = rows // parts
    where = jnp.stack([lax.axis_index("dap"), lax.axis_index("rep")]).astype(jnp.int32)
    gain_in, bias_in = input_gain[None], input_bias[None]
    all_gates = from_peers(gate_weight.T)
    both = project(
        where,
        residue_mask,
        pair_rep,
        [left_proj.T, left_gate.T, right_proj.T, right_gate.T],
        gain_in,
        bias_in,
        pair_mask,
        256,
    )
    both, all_gates = lax.optimization_barrier((both, all_gates))
    both = exchange(both, "dap")
    both, all_gates, out_weight = lax.optimization_barrier((both, all_gates, out_weight))
    gating = gates(where, pair_rep, all_gates, gain_in, bias_in, share, 256)

    def arrival(values):
        per = values.shape[0] // parts
        return jnp.swapaxes(values.reshape(parts, per, *values.shape[1:]), 0, 1).reshape(
            values.shape
        )

    product = exchange(products(both, share, (24, 8)), everyone)
    update = updates(
        product,
        gating,
        arrival(output_gain)[None],
        arrival(output_bias)[None],
        arrival(out_weight).T,
        256,
    )
    update = exchange(update.reshape(total // share, -1, lane), everyone)
    return jnp.swapaxes(place(update, share), 1, 2)


def solution(mesh):
    in_specs = (
        P("dap", None, None),
        P(),
        P("dap", None),
        P(),
        P(),
        P(None, "rep"),
        P(None, "rep"),
        P(None, "rep"),
        P(None, "rep"),
        P(None, "rep"),
        P(),
        P(),
        P(),
    )
    out_specs = P("rep", None, "dap")
    return jax.shard_map(
        on_device, mesh=mesh, in_specs=in_specs, out_specs=out_specs, check_vma=False
    )
```

```python
import functools

import jax
import jax.numpy as jnp
from jax import lax
from jax.experimental import pallas as pl
from jax.experimental.pallas import tpu as pltpu
from jax.sharding import PartitionSpec as P

eps = 1e-05
bf16 = jnp.bfloat16
f32 = jnp.float32
everyone = ("dap", "rep")
lane = 128
pack = 4


def params(mib):
    return pltpu.CompilerParams(vmem_limit_bytes=mib * 2**20)


def stay(array):
    return pltpu.with_memory_space_constraint(array, pltpu.HBM)


def near(array):
    return pltpu.with_memory_space_constraint(array, pltpu.VMEM)


whole = pl.BlockSpec(memory_space=pltpu.VMEM)


def rows_by_rows(a, b):
    return lax.dot_general(a, b, (((1,), (1,)), ((), ())), preferred_element_type=f32)


def column(row):
    return jnp.broadcast_to(row, (lane, lane)).T


def widen(column, tile):
    return column if tile == lane else jnp.concatenate([column] * (tile // lane), -1)


def centring(width):
    row = lax.broadcasted_iota(jnp.int32, (width, width), 0)
    at = lax.broadcasted_iota(jnp.int32, (width, width), 1)
    return ((row == at).astype(f32) - 1.0 / width).astype(bf16)


def normed_columns(x, gain, bias):
    width = x.shape[1]
    centred = rows_by_rows(centring(width), x)
    var = jnp.sum(centred * centred, axis=0, keepdims=True) * (1.0 / width)
    return (centred * lax.rsqrt(var + eps) * gain + bias).astype(bf16)


def project_kernel(
    where,
    residues,
    x_ref,
    left_proj,
    left_gate,
    right_proj,
    right_gate,
    gain_ref,
    bias_ref,
    keep_ref,
    mask_ref,
    out_ref,
    held,
):
    rows, tile, width = x_ref.shape
    hidden = out_ref.shape[0]
    step = rows + 1
    begin = pl.program_id(0) * tile
    weights = jnp.concatenate(
        [left_proj[...], left_gate[...], right_proj[...], right_gate[...]], 0
    )
    lanes = mask_ref[...].astype(f32)
    gain = widen(column(gain_ref[...]), tile)
    bias = widen(column(bias_ref[...]), tile)
    first = where[0] * rows
    for i in range(rows):
        y = jnp.dot(weights, normed_columns(x_ref[i], gain, bias), preferred_element_type=f32)
        keep = keep_ref[i : i + 1, :].astype(f32) * lanes * residues[first + i].astype(f32)
        half = keep * 0.5
        for side in range(2):
            linear = y[2 * side * hidden : (2 * side + 1) * hidden]
            gate = y[(2 * side + 1) * hidden : (2 * side + 2) * hidden]
            result = (jnp.tanh(gate * 0.5) + 1.0) * (linear * half)
            for part in range(tile // lane):
                held[side, part, pl.ds(i, hidden, stride=step), :] = result[
                    :, part * lane : (part + 1) * lane
                ]
    for side in range(2):
        for part in range(tile // lane):
            for c in range(hidden):
                across = pl.ds(pl.multiple_of(begin + part * lane, lane), lane)
                out_ref[c, side, :, across] = held[side, part, pl.ds(c * step, rows), :].astype(
                    bf16
                )


def project(where, residue_mask, pair_rep, weights, gain, bias, pair_mask, tile):
    rows, total, width = pair_rep.shape
    hidden = weights[0].shape[0]

    def fixed(t, *_):
        return (0, 0)

    return pl.pallas_call(
        project_kernel,
        grid_spec=pltpu.PrefetchScalarGridSpec(
            num_scalar_prefetch=2,
            grid=(total // tile,),
            in_specs=[
                pl.BlockSpec((rows, tile, width), lambda t, *_: (0, t, 0)),
                *[pl.BlockSpec((hidden, width), fixed)] * 4,
                *[pl.BlockSpec((1, width), fixed)] * 2,
                pl.BlockSpec((rows, tile), lambda t, *_: (0, t)),
                pl.BlockSpec((1, tile), lambda t, *_: (0, t)),
            ],
            out_specs=whole,
            scratch_shapes=[pltpu.VMEM((2, tile // lane, hidden * (rows + 1), lane), f32)],
        ),
        out_shape=pltpu.VMEM((hidden, 2, rows, total), bf16),
        compiler_params=params(32),
        name="project",
    )(
        where,
        residue_mask,
        stay(pair_rep),
        *[stay(w) for w in weights],
        stay(gain),
        stay(bias),
        stay(pair_mask),
        stay(residue_mask[None]),
    )


def gate_kernel(where, x_ref, w0, w1, w2, w3, gain_ref, bias_ref, out_ref, held):
    share, tile, _ = x_ref.shape
    channels = out_ref.shape[0]
    parts = (w0, w1, w2, w3)
    each = channels // len(parts)
    step = share + 1
    gain = widen(column(gain_ref[...]), tile)
    bias = widen(column(bias_ref[...]), tile)
    weights = jnp.concatenate([part[...] for part in parts], 0)
    for i in range(share):
        y = jnp.dot(weights, normed_columns(x_ref[i], gain, bias), preferred_element_type=f32)
        result = 0.5 * jnp.tanh(0.5 * y) + 0.5
        for shift in range(len(parts)):
            high, low = lax.div(where[1], 2), lax.rem(where[1], 2)
            owner = 2 * (1 - high if shift & 2 else high) + (1 - low if shift & 1 else low)
            for part in range(tile // lane):
                held[part, pl.ds(owner * (each * step) + i, each, stride=step), :] = result[
                    shift * each : (shift + 1) * each, part * lane : (part + 1) * lane
                ]
    for part in range(tile // lane):
        for c in range(channels):
            out_ref[c, :, part * lane : (part + 1) * lane] = held[
                part, pl.ds(c * step, share), :
            ].astype(bf16)


def gates(where, pair_rep, weights, gain, bias, share, tile):
    _, total, width = pair_rep.shape
    each = weights[0].shape[0]
    channels = each * len(weights)
    return pl.pallas_call(
        gate_kernel,
        grid_spec=pltpu.PrefetchScalarGridSpec(
            num_scalar_prefetch=1,
            grid=(total // tile,),
            in_specs=[
                pl.BlockSpec((share, tile, width), lambda t, where: (where[1], t, 0)),
                *[pl.BlockSpec((each, width), lambda t, where: (0, 0))] * len(weights),
                *[pl.BlockSpec((1, width), lambda t, where: (0, 0))] * 2,
            ],
            out_specs=pl.BlockSpec((None, channels, share, tile), lambda t, where: (t, 0, 0, 0)),
            scratch_shapes=[pltpu.VMEM((tile // lane, channels * (share + 1), lane), f32)],
        ),
        out_shape=pltpu.HBM((total // tile, channels, share, tile), bf16),
        compiler_params=params(16),
        cost_estimate=pl.CostEstimate(
            flops=2 * share * total * width * channels,
            bytes_accessed=4 * share * total * width,
            transcendentals=share * total * channels,
        ),
        name="gates",
    )(where, stay(pair_rep), *weights, stay(gain), stay(bias))


def product_kernel(both_ref, out_hbm, out_ref, sems, *, counts):
    blocks, _, rows, total = both_ref.shape
    share = out_ref.shape[1]
    copies, begin = [], 0
    for number, count in enumerate(counts):
        left = both_ref[begin : begin + count, 0].reshape(-1, total)
        right = both_ref[:, 1].reshape(-1, total)
        at = pl.ds(begin * rows // share, count * rows // share)
        out_ref[at] = rows_by_rows(left, right).astype(bf16).reshape(-1, share, total)
        copies.append(pltpu.make_async_copy(out_ref.at[at], out_hbm.at[at], sems.at[number]))
        copies[-1].start()
        begin += count
    for copy in copies:
        copy.wait()


def products(both, share, counts):
    blocks, _, rows, total = both.shape
    shape = (blocks * rows // share, share, total)
    return pl.pallas_call(
        functools.partial(product_kernel, counts=counts),
        in_specs=[whole],
        out_specs=pl.BlockSpec(memory_space=pltpu.HBM),
        out_shape=pltpu.HBM(shape, bf16),
        scratch_shapes=[pltpu.VMEM(shape, bf16), pltpu.SemaphoreType.DMA((len(counts),))],
        compiler_params=params(20),
        name="products",
    )(near(both))


def update_kernel(
    p_ref, gate_hbm, gain_ref, bias_ref, w_ref, out_ref, gate_ref, spread, gains, biases, sems, *, tile
):
    hidden, share, total = p_ref.shape
    channels = gate_ref.shape[1]
    span = lane // pack
    starts = range(0, total, tile)
    copies = [
        pltpu.make_async_copy(gate_hbm.at[number], gate_ref.at[number], sems.at[number])
        for number in range(len(starts))
    ]
    for copy in copies:
        copy.start()
    wide = (hidden, hidden * share)
    source = lax.broadcasted_iota(jnp.int32, wide, 0) * share
    target = lax.broadcasted_iota(jnp.int32, wide, 1)
    repeat = jnp.logical_and(target >= source, target < source + share)
    along = jnp.dot(w_ref[...], repeat.astype(bf16), preferred_element_type=f32)
    row = lax.broadcasted_iota(jnp.int32, (1, share, hidden * share), 1)
    place = lax.broadcasted_iota(jnp.int32, (1, share, hidden * share), 2)
    own = (lax.rem(place, share) == row).astype(f32)
    spread[...] = (along[:, None, :] * own).reshape(spread.shape).astype(bf16)
    gains[...] = jnp.broadcast_to(column(gain_ref[...])[:, None, :], gains.shape)
    biases[...] = jnp.broadcast_to(column(bias_ref[...])[:, None, :], biases.shape)

    def project_tile(begin):
        values = p_ref[:, :, begin : begin + tile].astype(f32)
        mean = jnp.sum(values, axis=0, keepdims=True) * (1.0 / hidden)
        centred = values - mean
        var = jnp.sum(centred * centred, axis=0, keepdims=True) * (1.0 / hidden)
        normed = centred * lax.rsqrt(var + eps) * widen(gains[...], tile) + widen(
            biases[...], tile
        )
        normed = normed.reshape(hidden * share, tile).astype(bf16)
        return jnp.dot(spread[...], normed, preferred_element_type=f32)

    def gate_tile(number, projected):
        gate = gate_ref[number].astype(f32).reshape(channels * share, tile)
        result = (gate * projected).reshape(channels // pack, pack, share, tile)
        for first in range(0, tile, span):
            piece = jnp.concatenate(
                [result[:, c, :, first : first + span] for c in range(pack)], axis=-1
            )
            out_ref[(starts[number] + first) // span] = piece.astype(bf16).reshape(
                out_ref.shape[1:]
            )

    ahead = min(2, len(starts))
    early = [project_tile(starts[number]) for number in range(ahead)]
    for copy in copies:
        copy.wait()
    for number in range(len(starts)):
        gate_tile(number, early[number] if number < ahead else project_tile(starts[number]))


def updates(product, gating, gain, bias, weights, tile):
    hidden, share, total = product.shape
    channels = gating.shape[1]
    span = lane // pack
    return pl.pallas_call(
        functools.partial(update_kernel, tile=tile),
        in_specs=[whole, pl.BlockSpec(memory_space=pltpu.HBM), whole, whole, whole],
        out_specs=whole,
        out_shape=pltpu.VMEM((total // span, channels * share // pack, lane), bf16),
        scratch_shapes=[
            pltpu.VMEM(gating.shape, bf16),
            pltpu.VMEM((channels * share, hidden * share), bf16),
            pltpu.VMEM((hidden, share, lane), f32),
            pltpu.VMEM((hidden, share, lane), f32),
            pltpu.SemaphoreType.DMA((total // tile,)),
        ],
        compiler_params=params(28),
        name="updates",
    )(near(product), stay(gating), gain, bias, weights)


def place_kernel(u_ref, out_hbm, out_ref, sems, *, share):
    blocks, rows, lanes = u_ref.shape
    copies = []
    for g in range(rows // share):
        flat = u_ref[:, g * share : (g + 1) * share, :].astype(f32).reshape(blocks * share, lanes)
        at = pl.ds(g * pack, pack)
        out_ref[at] = flat.T.astype(bf16).reshape(pack, lanes // pack, blocks * share)
        copies.append(pltpu.make_async_copy(out_ref.at[at], out_hbm.at[at], sems.at[g]))
        copies[-1].start()
    for copy in copies:
        copy.wait()


def place(received, share):
    blocks, rows, lanes = received.shape
    shape = (rows // share * pack, lanes // pack, blocks * share)
    return pl.pallas_call(
        functools.partial(place_kernel, share=share),
        in_specs=[whole],
        out_specs=pl.BlockSpec(memory_space=pltpu.HBM),
        out_shape=pltpu.HBM(shape, bf16),
        scratch_shapes=[pltpu.VMEM(shape, bf16), pltpu.SemaphoreType.DMA((rows // share,))],
        compiler_params=params(20),
        name="place",
    )(near(received))


def exchange(blocks, axes):
    return lax.all_to_all(blocks, axes, split_axis=0, concat_axis=0, tiled=True)


def from_peers(own):
    return [own] + [
        lax.ppermute(own, "rep", [(k, k ^ distance) for k in range(4)]) for distance in (1, 2, 3)
    ]


def on_device(
    pair_rep,
    residue_mask,
    pair_mask,
    input_gain,
    input_bias,
    left_proj,
    left_gate,
    right_proj,
    right_gate,
    gate_weight,
    output_gain,
    output_bias,
    out_weight,
):
    rows, total, _ = pair_rep.shape
    parts = lax.axis_size("rep")
    share = rows // parts
    where = jnp.stack([lax.axis_index("dap"), lax.axis_index("rep")]).astype(jnp.int32)
    gain_in, bias_in = input_gain[None], input_bias[None]
    all_gates = from_peers(gate_weight.T)
    both = project(
        where,
        residue_mask,
        pair_rep,
        [left_proj.T, left_gate.T, right_proj.T, right_gate.T],
        gain_in,
        bias_in,
        pair_mask,
        256,
    )
    both, all_gates = lax.optimization_barrier((both, all_gates))
    both = exchange(both, "dap")
    both, all_gates, out_weight = lax.optimization_barrier((both, all_gates, out_weight))
    gating = gates(where, pair_rep, all_gates, gain_in, bias_in, share, 256)

    def arrival(values):
        per = values.shape[0] // parts
        return jnp.swapaxes(values.reshape(parts, per, *values.shape[1:]), 0, 1).reshape(
            values.shape
        )

    product = exchange(products(both, share, (28, 4)), everyone)
    update = updates(
        product,
        gating,
        arrival(output_gain)[None],
        arrival(output_bias)[None],
        arrival(out_weight).T,
        256,
    )
    update = exchange(update.reshape(total // share, -1, lane), everyone)
    return jnp.swapaxes(place(update, share), 1, 2)


def solution(mesh):
    in_specs = (
        P("dap", None, None),
        P(),
        P("dap", None),
        P(),
        P(),
        P(None, "rep"),
        P(None, "rep"),
        P(None, "rep"),
        P(None, "rep"),
        P(None, "rep"),
        P(),
        P(),
        P(),
    )
    out_specs = P("rep", None, "dap")
    return jax.shard_map(
        on_device, mesh=mesh, in_specs=in_specs, out_specs=out_specs, check_vma=False
    )
```
